32 devices in a mesh: seq: 8 (over y, x, core), tensor: 4 (over z).
Axes of the slice: x: 2, y: 2, z: 4, core: 2. Of those that a mesh axis runs over, the one named last changes fastest.
Arguments:
- inputs: bfloat16 [32768, 2048], P('seq', 'tensor'), may hold values from -6 to 6
- out_grad: bfloat16 [32768, 2048], P('seq', 'tensor'), may hold values from -6 to 6
- router_score: float32 [32768], P('seq'), may hold values from 0.1 to 1
- route_index: int32 [8, 512], P('seq'), may hold values from 0 to 4095, as said below
- block_count: int32 [8], P('seq'), may hold values from 1 to 4, 16 in all
- w_in: bfloat16 [2048, 8192], P('seq', 'tensor'), may hold values from -0.125 to 0.125
- w_out: bfloat16 [8192, 2048], P('tensor', 'seq'), may hold values from -0.0625 to 0.0625
Outputs:
- input_grad: bfloat16 [32768, 2048], P('seq', 'tensor')
- score_grad: float32 [32768], P('seq')
The draws below stay inside these ranges and needn't reach their ends.
Inputs may be any that keep to these rules, and one draw needn't show every extreme that they name: `route_index`: row j holds 512 distinct positions within shard j; its first block_count[j] * 128 entries are the routed tokens, the rest padding. `block_count`: the counts sum to exactly 16.
All inputs are finite; a program needn't handle non-finite values.
Results may differ from the reference program's by a relative error of at most 0.012.
Values may be sent and summed in bfloat16 or wider, within the bound.
A program may use at most 128 MiB of HBM per device.

```python
import math
import jax
import jax.numpy as jnp
import numpy as np
from jax import lax

D = 2048
FF = 8192
TOK_DEV = 4096
BLK = 128
SHARDS = 8
TOKENS = 32768
AVG_BLOCKS = 2
CAP_BLOCKS = 4


def draw_route_index(key, part):
    shard_keys = jax.random.split(key, SHARDS)

    def one_shard(shard_key):
        return jax.random.permutation(shard_key, TOK_DEV)[:CAP_BLOCKS * BLK].astype(jnp.int32)
    return jax.vmap(one_shard)(shard_keys)


def shard_levels(rng, dims, cuts, smallest, top_value):
    def one(axis_at, blocks):
        steps = jax.random.uniform(jax.random.fold_in(jax.random.fold_in(rng, 6), axis_at), (blocks,), jnp.float32, smallest / len(cuts), top_value / len(cuts))
        return jnp.repeat(jnp.exp(steps), dims[axis_at] // blocks).reshape((-1,) + (1,) * (len(dims) - axis_at - 1))

    loudness = one(*cuts[0])
    for cut in cuts[1:]:
        loudness = loudness * one(*cut)
    return loudness


def length_profile(number_of, total, limit, skew):
    loads = [(1 << 20) // math.isqrt(standing ** skew) + 1 for standing in range(2, number_of + 1)]
    rest, holding = total - limit - (number_of - 1), [1] * (number_of - 1)
    while rest > 0:
        free = [i for i in range(number_of - 1) if holding[i] < limit]
        whole, remaining = sum([loads[i] for i in free]), rest
        for i in free:
            more = min(limit - holding[i], max(1, remaining * loads[i] // whole), rest)
            holding[i] = holding[i] + more
            rest = rest - more
    return np.array([limit] + holding)


def ragged_sizes(key, number_of, total, reach, skew):
    if number_of == 2:
        one = jax.random.randint(key, (), max(1, total - reach), min(reach, total - 1) + 1)
        return jnp.stack([one, total - one])
    sizes = jnp.asarray(length_profile(number_of, total, reach, skew), jnp.int32)
    couples = (number_of - 1) // 2
    giver, sink = sizes[1:1 + 2 * couples:2], sizes[2:2 + 2 * couples:2]
    room = jnp.minimum(giver - 1, reach - sink)
    passed = jax.random.randint(jax.random.fold_in(key, 1), (couples,), 0, 1 << 20) % (room + 1)
    sizes = sizes.at[1:1 + 2 * couples:2].set(giver - passed).at[2:2 + 2 * couples:2].set(sink + passed)
    return sizes[jax.random.permutation(jax.random.fold_in(key, 2), number_of)]


def gaussian(stream_key, extent, width, reach, cuts=(), kind=jnp.bfloat16):
    result = jax.random.normal(stream_key, extent, jnp.float32) * width
    if len(cuts) > 0:
        result = shard_levels(stream_key, extent, cuts, -0.22, 0.18) * result
    return jnp.clip(result, min=-reach, max=reach).astype(kind)


def setup_inputs(seed: int = 0) -> dict:
    key_of = jax.random.split(jax.random.key(seed), 8)
    return {
        "inputs": gaussian(key_of[0], (TOKENS, D), 1.0, 6.0, ((0, 8), (1, 4))),
        "out_grad": gaussian(key_of[1], (TOKENS, D), 1.0, 6.0, ((0, 8), (1, 4))),
        "router_score": jnp.clip(0.1 + 0.9 * jax.random.uniform(key_of[2], (TOKENS,), jnp.float32) ** shard_levels(key_of[2], (TOKENS,), ((0, 8),), -0.2, 0.2), 0.1, 1.0),
        "route_index": draw_route_index(jax.random.fold_in(key_of[7], 71), 0),
        "block_count": ragged_sizes(key_of[4], SHARDS, SHARDS * AVG_BLOCKS, CAP_BLOCKS, 2).astype(jnp.int32),
        "w_in": gaussian(key_of[5], (D, FF), D ** -0.5, 0.125, ((0, 8), (1, 4))),
        "w_out": gaussian(key_of[6], (FF, D), FF ** -0.5, 0.0625, ((0, 4), (1, 8))),
    }


gelu_coeff = 0.7978845608028654
cubic_coeff = 0.044715


def gelu_pair(values):
    inner = gelu_coeff * (values + cubic_coeff * values * values * values)
    tangent = jnp.tanh(inner)
    forward = 0.5 * values * (1.0 + tangent)
    slope = 0.5 * (1.0 + tangent) + 0.5 * values * (1.0 - tangent * tangent) * gelu_coeff * (1.0 + 3.0 * cubic_coeff * values * values)
    return forward, slope


def round_keep(values):
    narrow = lax.optimization_barrier(values.astype(jnp.bfloat16))
    return narrow.astype(jnp.float32)


def reference(inputs, out_grad, router_score, route_index, block_count, w_in, w_out):
    route_rows = CAP_BLOCKS * BLK
    live_total = SHARDS * AVG_BLOCKS * BLK
    step_rows = AVG_BLOCKS * BLK
    counts = block_count.astype(jnp.int32)
    offsets = (jnp.cumsum(counts) - counts).astype(jnp.int32)
    slot_ids = jnp.arange(route_rows, dtype=jnp.int32)
    target = offsets[:, None] * BLK + slot_ids[None, :]
    is_live = slot_ids[None, :] < (counts * BLK)[:, None]
    target = jnp.where(is_live, target, live_total).astype(jnp.int32)
    shard_ids = jnp.arange(SHARDS, dtype=jnp.int32)
    source = (shard_ids[:, None] * TOK_DEV + route_index).astype(jnp.int32)
    gathered = jnp.zeros((live_total,), jnp.int32).at[target.reshape(-1)].set(source.reshape(-1), mode="drop")
    weight_in = w_in.astype(jnp.float32)
    weight_out = w_out.astype(jnp.float32)

    def one_step(picked):
        chosen = inputs[picked].astype(jnp.float32)
        grads = out_grad[picked].astype(jnp.float32)
        scores = router_score[picked].astype(jnp.float32)
        hidden = jnp.dot(chosen, weight_in)
        forward, slope = gelu_pair(hidden)
        active = round_keep(forward)
        upstream = jnp.dot(grads, weight_out.T)
        score_part = jnp.sum(upstream * active, axis=1)
        hidden_grad = round_keep(scores[:, None] * upstream * slope)
        input_part = jnp.dot(hidden_grad, weight_in.T).astype(jnp.bfloat16)
        return input_part, score_part

    input_rows, score_rows = lax.map(one_step, gathered.reshape(-1, step_rows))
    input_grad = jnp.zeros((TOKENS, D), jnp.bfloat16).at[gathered].set(input_rows.reshape(-1, D))
    score_grad = jnp.zeros((TOKENS,), jnp.float32).at[gathered].set(score_rows.reshape(-1).astype(jnp.float32))
    return input_grad, score_grad
```

```python
import functools

import jax
import jax.numpy as jnp
from jax import lax
from jax.experimental import pallas as pl
from jax.experimental.pallas import tpu as pltpu
from jax.sharding import PartitionSpec as P

BLK = 128
MESH = pl.DeviceIdType.MESH
F32, BF16 = jnp.float32, jnp.bfloat16
NT = (((1,), (1,)), ((), ()))
NN = (((1,), (0,)), ((), ()))

gelu_coeff = 0.7978845608028654
cubic_coeff = 0.044715


def gelu_pair(values):
    square = values * values
    tangent = jnp.tanh(gelu_coeff * (values + cubic_coeff * square * values))
    half = 0.5 * (1.0 + tangent)
    slope = half + 0.5 * values * (1.0 - tangent * tangent) * gelu_coeff * (
        1.0 + 3.0 * cubic_coeff * square
    )
    return values * half, slope


def dot(a, b, dims):
    return lax.dot_general(a, b, dims, preferred_element_type=F32)


def heavy_kernel(
    n, nt, idx_ref, inputs_ref, grads_ref, win_ref, wout_ref, rows_ref, score_ref,
    tok_buf, x_buf, g_buf, win_buf, wout_buf, act_buf, slope_buf, hg_buf,
    pair_send, pair_recv, z_send, z_recv, own_buf, sc_out, sc_pair, sc_z,
    tok_sem, wl_sem, w_send, w_recv, z_ssem, z_rsem, p_ssem, p_rsem,
    os_sem, or_sem, oz_ssem, oz_rsem, ss_sem, sr_sem,
):
    s, t = lax.axis_index("seq"), lax.axis_index("tensor")
    c, k = lax.div(s, 2), lax.rem(s, 2)
    chips = n // 2
    toks, width = inputs_ref.shape
    rows = idx_ref.shape[1]
    depth = win_ref.shape[0]
    half = win_ref.shape[1] // 2
    other = 1 - k
    partner = c * 2 + other
    square = chips == 4

    if square:
        out_chip = [c + 1 - 2 * lax.rem(c, 2), lax.rem(c + 2, 4), 3 - c]
        in_chip = out_chip
    else:
        out_chip = [lax.rem(c + r, chips) for r in range(1, chips)]
        in_chip = [lax.rem(c + chips - r, chips) for r in range(1, chips)]

    def t_out(r):
        return lax.rem(t + r, nt)

    def t_in(r):
        return lax.rem(t + nt - r, nt)

    load = [
        pltpu.make_async_copy(src, tok_buf.at[i], tok_sem.at[i])
        for i, src in enumerate((inputs_ref, grads_ref))
    ]
    for cp in load:
        cp.start()

    def weight_src(w, core):
        start = pl.multiple_of(core * half, half)
        if w == 0:
            return win_ref.at[:, pl.ds(start, half)]
        return wout_ref.at[pl.ds(start, half), :]

    def weight_dst(w, owner):
        if w == 0:
            return win_buf.at[pl.ds(pl.multiple_of(owner * depth, depth), depth), :]
        return wout_buf.at[owner]

    local = [
        pltpu.make_async_copy(weight_src(w, k), weight_dst(w, s), wl_sem.at[w]) for w in range(2)
    ]
    for cp in local:
        cp.start()

    barrier = pltpu.get_barrier_semaphore()
    for chip in out_chip:
        for core in range(2):
            pl.semaphore_signal(
                barrier, inc=1, device_id={"seq": chip * 2 + core}, device_id_type=MESH
            )
    pl.semaphore_signal(barrier, inc=1, device_id={"seq": partner}, device_id_type=MESH)
    for r in range(1, nt):
        pl.semaphore_signal(barrier, inc=1, device_id={"tensor": t_out(r)}, device_id_type=MESH)
    pl.semaphore_wait(barrier, 2 * (chips - 1) + 1 + nt - 1)

    def weight_copy(w, r, q):
        core = k if q == 0 else other
        return pltpu.make_async_remote_copy(
            src_ref=weight_src(w, core), dst_ref=weight_dst(w, s),
            send_sem=w_send.at[w, r, q], recv_sem=w_recv.at[w, r, q],
            device_id={"seq": out_chip[r] * 2 + core}, device_id_type=MESH,
        )

    def weight_hop(w, q):
        came, go = (0, 1) if q == 0 else (1, 0)
        owner = in_chip[came] * 2 + (k if q == 0 else other)
        return pltpu.make_async_remote_copy(
            src_ref=weight_dst(w, owner), dst_ref=weight_dst(w, owner),
            send_sem=w_send.at[w, 2, q], recv_sem=w_recv.at[w, 2, q],
            device_id={"seq": out_chip[go] * 2 + k}, device_id_type=MESH,
        )

    def weight_landed(w, r, q):
        owner = in_chip[r] * 2 + (k if q == 0 else other)
        return pltpu.make_async_remote_copy(
            src_ref=weight_dst(w, owner), dst_ref=weight_dst(w, owner),
            send_sem=w_send.at[w, r, q], recv_sem=w_recv.at[w, r, q],
            device_id={"seq": owner}, device_id_type=MESH,
        )

    def weight_pair(w, owner):
        return pltpu.make_async_remote_copy(
            src_ref=weight_src(w, other), dst_ref=weight_dst(w, owner),
            send_sem=w_send.at[w, chips - 1, 0], recv_sem=w_recv.at[w, chips - 1, 0],
            device_id={"seq": partner}, device_id_type=MESH,
        )

    direct = range(2) if square else range(chips - 1)

    def start_weights(w):
        for q in range(2):
            for r in direct:
                weight_copy(w, r, q).start()
        weight_pair(w, s).start()

    def pass_weights(w):
        if square:
            for q in range(2):
                weight_landed(w, q, q).wait_recv()
                weight_hop(w, q).start()

    def finish_weights(w):
        local[w].wait()
        weight_pair(w, partner).wait_recv()
        for r in range(chips - 1):
            for q in range(2):
                if square and r == q:
                    continue
                weight_landed(w, r, q).wait_recv()

    def drain_weights(w):
        weight_pair(w, s).wait_send()
        for q in range(2):
            for r in direct:
                weight_copy(w, r, q).wait_send()
            if square:
                weight_hop(w, q).wait_send()

    tokens = (x_buf, g_buf)

    def piece(v, shard, column):
        return tokens[v].at[shard, :, pl.ds(pl.multiple_of(column * width, width), width)]

    def gather(v):
        load[v].wait()
        step = min(512, toks)
        column = jnp.transpose(jnp.broadcast_to(idx_ref[...], (128, rows)))[:, :1]
        dst = piece(v, k, t)
        total = jnp.zeros((rows, width), F32)
        x_own = own_buf

        x_own[...] = total

        def body(i, carry):
            start = pl.multiple_of(i * step, step)
            spots = lax.broadcasted_iota(jnp.int32, (rows, step), 1) + i * step
            hot = jnp.where(column == spots, 1.0, 0.0).astype(BF16)
            x_own[...] += dot(hot, tok_buf[v, pl.ds(start, step), :], NN)
            return carry

        lax.fori_loop(0, toks // step, body, 0)
        dst[...] = x_own[...].astype(BF16)

    def z_copy(v, r):
        return pltpu.make_async_remote_copy(
            src_ref=piece(v, k, t), dst_ref=piece(v, k, t),
            send_sem=z_ssem.at[v, r], recv_sem=z_rsem.at[v, r],
            device_id={"tensor": t_out(r)}, device_id_type=MESH,
        )

    def z_landed(v, r):
        return pltpu.make_async_remote_copy(
            src_ref=piece(v, k, t_in(r)), dst_ref=piece(v, k, t_in(r)),
            send_sem=z_ssem.at[v, r], recv_sem=z_rsem.at[v, r],
            device_id={"tensor": t_in(r)}, device_id_type=MESH,
        )

    def pair_copy(v, r, shard):
        return pltpu.make_async_remote_copy(
            src_ref=piece(v, shard, t_in(r)), dst_ref=piece(v, shard, t_in(r)),
            send_sem=p_ssem.at[v, r], recv_sem=p_rsem.at[v, r],
            device_id={"seq": partner}, device_id_type=MESH,
        )

    def start_tokens(v):
        for r in range(1, nt):
            z_copy(v, r).start()
        pair_copy(v, 0, k).start()

    def pass_tokens(v):
        for r in range(1, nt):
            z_landed(v, r).wait_recv()
            pair_copy(v, r, k).start()

    def finish_tokens(v):
        for r in range(nt):
            pair_copy(v, r, other).wait_recv()

    def drain_tokens(v):
        for r in range(1, nt):
            z_copy(v, r).wait_send()
        for r in range(nt):
            pair_copy(v, r, k).wait_send()

    start_weights(0)
    gather(0)
    start_tokens(0)
    gather(1)
    pass_weights(0)
    start_weights(1)
    pass_tokens(0)
    start_tokens(1)
    finish_weights(0)
    finish_tokens(0)

    ft = min(256, half)

    def hidden_step(i, carry):
        shard, f = lax.div(i, half // ft), lax.rem(i, half // ft)
        cols = pl.ds(pl.multiple_of(f * ft, ft), ft)
        hidden = dot(x_buf[shard], win_buf[:, cols], NN)
        forward, slope = gelu_pair(hidden)
        act_buf[shard, :, cols] = forward.astype(BF16)
        slope_buf[shard, :, cols] = slope
        return carry

    lax.fori_loop(0, 2 * (half // ft), hidden_step, 0)

    pass_weights(1)
    pass_tokens(1)
    finish_weights(1)
    finish_tokens(1)

    def upstream(shard):
        sc_out[...] = jnp.zeros_like(sc_out)

        def step(f, carry):
            cols = pl.ds(pl.multiple_of(f * ft, ft), ft)
            weights = jnp.concatenate([wout_buf[i, cols, :] for i in range(n)], axis=1)
            up = dot(g_buf[shard], weights, NT)
            hg_buf[:, cols] = (up * slope_buf[shard, :, cols]).astype(BF16)
            terms = up * act_buf[shard, :, cols].astype(F32)
            part = terms[:, :128]
            for i in range(1, ft // 128):
                part = part + terms[:, i * 128:(i + 1) * 128]
            sc_out[...] += part
            return carry

        lax.fori_loop(0, half // ft, step, 0)
        line = jnp.sum(jnp.transpose(sc_out[...]), axis=0, keepdims=True)
        return jnp.broadcast_to(line, (8, rows))

    def grads_of(column):
        span = pl.ds(pl.multiple_of(column * width, width), width)
        return dot(hg_buf[...], win_buf[span, :], NT)

    def o_pair(r):
        return pltpu.make_async_remote_copy(
            src_ref=pair_send.at[r], dst_ref=pair_recv.at[r],
            send_sem=os_sem.at[r], recv_sem=or_sem.at[r],
            device_id={"seq": partner}, device_id_type=MESH,
        )

    def o_z(r):
        return pltpu.make_async_remote_copy(
            src_ref=z_send.at[r - 1], dst_ref=z_recv.at[r - 1],
            send_sem=oz_ssem.at[r], recv_sem=oz_rsem.at[r],
            device_id={"tensor": t_out(r)}, device_id_type=MESH,
        )

    def s_pair():
        return pltpu.make_async_remote_copy(
            src_ref=sc_pair.at[0], dst_ref=sc_pair.at[1],
            send_sem=ss_sem.at[0], recv_sem=sr_sem.at[0],
            device_id={"seq": partner}, device_id_type=MESH,
        )

    def s_z(r):
        return pltpu.make_async_remote_copy(
            src_ref=sc_z.at[0], dst_ref=sc_z.at[r],
            send_sem=ss_sem.at[r], recv_sem=sr_sem.at[r],
            device_id={"tensor": t_out(r)}, device_id_type=MESH,
        )

    order = list(range(1, nt)) + [0]
    sc_pair[0] = upstream(other)
    s_pair().start()
    for r in order:
        pair_send[r] = grads_of(t_out(r)).astype(BF16)
        o_pair(r).start()

    mine = upstream(k)
    s_pair().wait_recv()
    sc_z[0] = mine + sc_pair[1]
    for r in range(1, nt):
        s_z(r).start()
    for r in order:
        part = grads_of(t_out(r))
        o_pair(r).wait_recv()
        part = part + pair_recv[r].astype(F32)
        if r == 0:
            own_buf[...] = part
        else:
            z_send[r - 1] = part.astype(BF16)
            o_z(r).start()

    drain_weights(0)
    drain_weights(1)
    drain_tokens(0)
    drain_tokens(1)
    s_pair().wait_send()
    for r in range(nt):
        o_pair(r).wait_send()
    for r in range(1, nt):
        s_z(r).wait()
    total = sc_z[0]
    for r in range(1, nt):
        total = total + sc_z[r]
    score_ref[...] = total
    for r in range(1, nt):
        o_z(r).wait()
    full = own_buf[...]
    for r in range(1, nt):
        full = full + z_recv[r - 1].astype(F32)
    rows_ref[...] = full.astype(BF16)


def scatter_kernel(count_ref, idx_ref, rows_ref, line_ref, score_ref, grad_ref, out_ref):
    tile = grad_ref.shape[0]
    slots = idx_ref.shape[1]
    live = lax.broadcasted_iota(jnp.int32, (1, slots), 1) < count_ref[0] * BLK
    picked = jnp.where(live, idx_ref[...], -1)
    spots = lax.broadcasted_iota(jnp.int32, (tile, slots), 0) + pl.program_id(0) * tile
    hot = jnp.where(spots == picked, 1.0, 0.0).astype(BF16)
    scale = jnp.transpose(jnp.broadcast_to(score_ref[...], (128, tile)))[:, :1]
    grad_ref[...] = (dot(hot, rows_ref[...], NN) * scale).astype(BF16)
    rest = jnp.broadcast_to(line_ref[:1, :], (16, slots))
    total = jnp.zeros((16, tile), F32)
    for _ in range(3):
        head = rest.astype(BF16)
        total = total + dot(head, hot, NT)
        rest = rest - head.astype(F32)
    out_ref[...] = total[:1, :]


def per_device(n, nt, inputs, out_grad, router_score, route_index, block_count, w_in, w_out):
    toks, width = inputs.shape
    rows = route_index.shape[1]
    depth, ff = w_in.shape
    half = ff // 2
    dim = width * nt
    chips = n // 2
    dma = pltpu.SemaphoreType.DMA
    vm = pl.BlockSpec(memory_space=pltpu.VMEM)
    hbm = pl.BlockSpec(memory_space=pl.ANY)
    row_grads, lines = pl.pallas_call(
        functools.partial(heavy_kernel, n, nt),
        out_shape=(
            jax.ShapeDtypeStruct((rows, width), BF16),
            jax.ShapeDtypeStruct((8, rows), F32),
        ),
        in_specs=[vm, hbm, hbm, hbm, hbm],
        out_specs=(vm, vm),
        scratch_shapes=[
            pltpu.VMEM((2, toks, width), BF16),
            pltpu.VMEM((2, rows, dim), BF16),
            pltpu.VMEM((2, rows, dim), BF16),
            pltpu.VMEM((n * depth, half), BF16),
            pltpu.VMEM((n, half, depth), BF16),
            pltpu.VMEM((2, rows, half), BF16),
            pltpu.VMEM((2, rows, half), F32),
            pltpu.VMEM((rows, half), BF16),
            pltpu.VMEM((nt, rows, width), BF16),
            pltpu.VMEM((nt, rows, width), BF16),
            pltpu.VMEM((nt - 1, rows, width), BF16),
            pltpu.VMEM((nt - 1, rows, width), BF16),
            pltpu.VMEM((rows, width), F32),
            pltpu.VMEM((rows, 128), F32),
            pltpu.VMEM((2, 8, rows), F32),
            pltpu.VMEM((nt, 8, rows), F32),
            dma((2,)), dma((2,)),
            dma((2, chips, 2)), dma((2, chips, 2)),
            dma((2, nt)), dma((2, nt)),
            dma((2, nt)), dma((2, nt)),
            dma((nt,)), dma((nt,)),
            dma((nt,)), dma((nt,)),
            dma((nt,)), dma((nt,)),
        ],
        compiler_params=pltpu.CompilerParams(
            collective_id=0, has_side_effects=True, vmem_limit_bytes=58 * 2**20
        ),
        name="heavy",
    )(route_index, inputs, out_grad, w_in, w_out)

    tile = min(1024, toks)
    input_grad, score_grad = pl.pallas_call(
        scatter_kernel,
        grid=(toks // tile,),
        out_shape=(
            jax.ShapeDtypeStruct((toks, width), BF16),
            jax.ShapeDtypeStruct((1, toks), F32),
        ),
        in_specs=[
            pl.BlockSpec(memory_space=pltpu.SMEM),
            pl.BlockSpec((1, rows), lambda i: (0, 0)),
            pl.BlockSpec((rows, width), lambda i: (0, 0)),
            pl.BlockSpec((8, rows), lambda i: (0, 0)),
            pl.BlockSpec((1, tile), lambda i: (0, i)),
        ],
        out_specs=(
            pl.BlockSpec((tile, width), lambda i: (i, 0)),
            pl.BlockSpec((1, tile), lambda i: (0, i)),
        ),
        compiler_params=pltpu.CompilerParams(vmem_limit_bytes=32 * 2**20),
        name="scatter",
    )(block_count, route_index, row_grads, lines, router_score.reshape(1, toks))
    return input_grad, score_grad.reshape(toks)


def solution(mesh):
    placed = (
        P("seq", "tensor"),
        P("seq", "tensor"),
        P("seq"),
        P("seq", None),
        P("seq"),
        P("seq", "tensor"),
        P("tensor", "seq"),
    )
    return jax.shard_map(
        functools.partial(per_device, mesh.shape["seq"], mesh.shape["tensor"]),
        mesh=mesh,
        in_specs=placed,
        out_specs=(P("seq", "tensor"), P("seq")),
        check_vma=False,
    )
```

```python
import functools

import jax
import jax.numpy as jnp
from jax import lax
from jax.experimental import pallas as pl
from jax.experimental.pallas import tpu as pltpu
from jax.sharding import PartitionSpec as P

BLK = 128
MESH = pl.DeviceIdType.MESH
F32, BF16 = jnp.float32, jnp.bfloat16
NT = (((1,), (1,)), ((), ()))
NN = (((1,), (0,)), ((), ()))

gelu_coeff = 0.7978845608028654
cubic_coeff = 0.044715


def gelu_pair(values):
    square = values * values
    tangent = jnp.tanh(gelu_coeff * (values + cubic_coeff * square * values))
    half = 0.5 * (1.0 + tangent)
    slope = half + 0.5 * values * (1.0 - tangent * tangent) * gelu_coeff * (
        1.0 + 3.0 * cubic_coeff * square
    )
    return values * half, slope


def dot(a, b, dims):
    return lax.dot_general(a, b, dims, preferred_element_type=F32)


def heavy_kernel(
    n, nt, idx_ref, inputs_ref, grads_ref, win_ref, wout_ref, rows_ref, score_ref,
    tok_buf, x_buf, g_buf, win_buf, wout_buf, act_buf, slope_buf, hg_buf,
    pair_send, pair_recv, z_send, z_recv, own_buf, keep, sc_out, sc_pair, sc_z,
    tok_sem, wl_sem, w_send, w_recv, z_ssem, z_rsem, p_ssem, p_rsem,
    os_sem, or_sem, oz_ssem, oz_rsem, ss_sem, sr_sem,
):
    s, t = lax.axis_index("seq"), lax.axis_index("tensor")
    c, k = lax.div(s, 2), lax.rem(s, 2)
    chips = n // 2
    toks, width = inputs_ref.shape
    rows = idx_ref.shape[1]
    depth = win_ref.shape[0]
    half = win_ref.shape[1] // 2
    other = 1 - k
    partner = c * 2 + other
    square = chips == 4

    if square:
        out_chip = [c + 1 - 2 * lax.rem(c, 2), lax.rem(c + 2, 4), 3 - c]
        in_chip = out_chip
    else:
        out_chip = [lax.rem(c + r, chips) for r in range(1, chips)]
        in_chip = [lax.rem(c + chips - r, chips) for r in range(1, chips)]

    def t_out(r):
        return lax.rem(t + r, nt)

    load = [
        pltpu.make_async_copy(src, tok_buf.at[i], tok_sem.at[i])
        for i, src in enumerate((inputs_ref, grads_ref))
    ]
    for cp in load:
        cp.start()

    def weight_src(w, core):
        start = pl.multiple_of(core * half, half)
        if w == 0:
            return win_ref.at[:, pl.ds(start, half)]
        return wout_ref.at[pl.ds(start, half), :]

    def weight_dst(w, owner):
        if w == 0:
            return win_buf.at[pl.ds(pl.multiple_of(owner * depth, depth), depth), :]
        return wout_buf.at[owner]

    local = [
        pltpu.make_async_copy(weight_src(w, k), weight_dst(w, s), wl_sem.at[w]) for w in range(2)
    ]
    for cp in local:
        cp.start()

    barrier = pltpu.get_barrier_semaphore()
    for chip in out_chip:
        for core in range(2):
            pl.semaphore_signal(
                barrier, inc=1, device_id={"seq": chip * 2 + core}, device_id_type=MESH
            )
    pl.semaphore_signal(barrier, inc=1, device_id={"seq": partner}, device_id_type=MESH)
    for r in range(1, nt):
        pl.semaphore_signal(barrier, inc=1, device_id={"tensor": t_out(r)}, device_id_type=MESH)
    pl.semaphore_wait(barrier, 2 * (chips - 1) + 1 + nt - 1)

    def weight_copy(w, r, q):
        core = k if q == 0 else other
        return pltpu.make_async_remote_copy(
            src_ref=weight_src(w, core), dst_ref=weight_dst(w, s),
            send_sem=w_send.at[w, r, q], recv_sem=w_recv.at[w, r, q],
            device_id={"seq": out_chip[r] * 2 + core}, device_id_type=MESH,
        )

    def weight_hop(w, q):
        came, go = (0, 1) if q == 0 else (1, 0)
        owner = in_chip[came] * 2 + (k if q == 0 else other)
        return pltpu.make_async_remote_copy(
            src_ref=weight_dst(w, owner), dst_ref=weight_dst(w, owner),
            send_sem=w_send.at[w, 2, q], recv_sem=w_recv.at[w, 2, q],
            device_id={"seq": out_chip[go] * 2 + k}, device_id_type=MESH,
        )

    def weight_landed(w, r, q):
        owner = in_chip[r] * 2 + (k if q == 0 else other)
        return pltpu.make_async_remote_copy(
            src_ref=weight_dst(w, owner), dst_ref=weight_dst(w, owner),
            send_sem=w_send.at[w, r, q], recv_sem=w_recv.at[w, r, q],
            device_id={"seq": owner}, device_id_type=MESH,
        )

    def weight_pair(w, owner):
        return pltpu.make_async_remote_copy(
            src_ref=weight_src(w, other), dst_ref=weight_dst(w, owner),
            send_sem=w_send.at[w, chips - 1, 0], recv_sem=w_recv.at[w, chips - 1, 0],
            device_id={"seq": partner}, device_id_type=MESH,
        )

    direct = range(2) if square else range(chips - 1)

    def start_weights(w):
        for q in range(2):
            for r in direct:
                weight_copy(w, r, q).start()
        weight_pair(w, s).start()

    def pass_weights(w):
        if square:
            for q in range(2):
                weight_landed(w, q, q).wait_recv()
                weight_hop(w, q).start()

    def finish_weights(w):
        local[w].wait()
        weight_pair(w, partner).wait_recv()
        for r in range(chips - 1):
            for q in range(2):
                if square and r == q:
                    continue
                weight_landed(w, r, q).wait_recv()

    def drain_weights(w):
        weight_pair(w, s).wait_send()
        for q in range(2):
            for r in direct:
                weight_copy(w, r, q).wait_send()
            if square:
                weight_hop(w, q).wait_send()

    tokens = (x_buf, g_buf)

    def piece(v, shard, column):
        return tokens[v].at[shard, :, pl.ds(pl.multiple_of(column * width, width), width)]

    def gather(v):
        load[v].wait()
        step = min(512, toks)
        column = jnp.transpose(jnp.broadcast_to(idx_ref[...], (128, rows)))[:, :1]
        dst = piece(v, k, t)
        total = jnp.zeros((rows, width), F32)
        x_own = own_buf

        x_own[...] = total

        def body(i, carry):
            start = pl.multiple_of(i * step, step)
            spots = lax.broadcasted_iota(jnp.int32, (rows, step), 1) + i * step
            hot = jnp.where(column == spots, 1.0, 0.0).astype(BF16)
            x_own[...] += dot(hot, tok_buf[v, pl.ds(start, step), :], NN)
            return carry

        lax.fori_loop(0, toks // step, body, 0)
        dst[...] = x_own[...].astype(BF16)

    def origin(way, d):
        return lax.rem(t + nt - d, nt) if way == 0 else lax.rem(t + d, nt)

    def has(way, d):
        return t >= d if way == 0 else t + d < nt

    def z_to(way):
        return lax.rem(t + 1, nt) if way == 0 else lax.rem(t + nt - 1, nt)

    def z_copy(v, way, d):
        ref = piece(v, k, origin(way, d))
        return pltpu.make_async_remote_copy(
            src_ref=ref, dst_ref=ref,
            send_sem=z_ssem.at[v, way, d], recv_sem=z_rsem.at[v, way, d + 1],
            device_id={"tensor": z_to(way)}, device_id_type=MESH,
        )

    def z_landed(v, way, d):
        ref = piece(v, k, origin(way, d))
        return pltpu.make_async_remote_copy(
            src_ref=ref, dst_ref=ref,
            send_sem=z_ssem.at[v, way, d], recv_sem=z_rsem.at[v, way, d],
            device_id={"tensor": z_to(1 - way)}, device_id_type=MESH,
        )

    def pair_copy(v, way, d, shard):
        ref = piece(v, shard, origin(way, d))
        return pltpu.make_async_remote_copy(
            src_ref=ref, dst_ref=ref,
            send_sem=p_ssem.at[v, way, d], recv_sem=p_rsem.at[v, way, d],
            device_id={"seq": partner}, device_id_type=MESH,
        )

    def start_tokens(v):
        for way in range(2):
            @pl.when(has(1 - way, 1))
            def _():
                z_copy(v, way, 0).start()
        pair_copy(v, 0, 0, k).start()

    def pass_tokens(v, d):
        for way in range(2):
            @pl.when(has(way, d))
            def _():
                z_landed(v, way, d).wait_recv()
                if d < nt - 1:
                    @pl.when(has(1 - way, 1))
                    def _():
                        z_copy(v, way, d).start()
                pair_copy(v, way, d, k).start()

    def finish_tokens(v):
        pair_copy(v, 0, 0, other).wait_recv()
        for way in range(2):
            for d in range(1, nt):
                @pl.when(has(way, d))
                def _():
                    pair_copy(v, way, d, other).wait_recv()

    def drain_tokens(v):
        pair_copy(v, 0, 0, k).wait_send()
        for way in range(2):
            for d in range(nt - 1):
                @pl.when(has(way, d) & has(1 - way, 1))
                def _():
                    z_copy(v, way, d).wait_send()
            for d in range(1, nt):
                @pl.when(has(way, d))
                def _():
                    pair_copy(v, way, d, k).wait_send()

    start_weights(0)
    gather(0)
    start_tokens(0)
    gather(1)
    start_tokens(1)
    pass_tokens(0, 1)
    pass_weights(0)
    start_weights(1)
    for d in range(2, nt):
        if d < nt - 1:
            pass_tokens(0, d)
        pass_tokens(1, d - 1)
    pass_weights(1)
    pass_tokens(0, nt - 1)
    finish_weights(0)
    finish_tokens(0)

    ft = min(256, half)

    def hidden_step(i, carry):
        shard, f = lax.div(i, half // ft), lax.rem(i, half // ft)
        cols = pl.ds(pl.multiple_of(f * ft, ft), ft)
        hidden = dot(x_buf[shard], win_buf[:, cols], NN)
        forward, slope = gelu_pair(hidden)
        act_buf[shard, :, cols] = forward.astype(BF16)
        slope_buf[shard, :, cols] = slope
        return carry

    lax.fori_loop(0, 2 * (half // ft), hidden_step, 0)

    pass_tokens(1, nt - 1)
    finish_weights(1)
    finish_tokens(1)

    def upstream(shard):
        sc_out[...] = jnp.zeros_like(sc_out)

        def step(f, carry):
            cols = pl.ds(pl.multiple_of(f * ft, ft), ft)
            weights = jnp.concatenate([wout_buf[i, cols, :] for i in range(n)], axis=1)
            up = dot(g_buf[shard], weights, NT)
            hg_buf[:, cols] = (up * slope_buf[shard, :, cols]).astype(BF16)
            terms = up * act_buf[shard, :, cols].astype(F32)
            part = terms[:, :128]
            for i in range(1, ft // 128):
                part = part + terms[:, i * 128:(i + 1) * 128]
            sc_out[...] += part
            return carry

        lax.fori_loop(0, half // ft, step, 0)
        line = jnp.sum(jnp.transpose(sc_out[...]), axis=0, keepdims=True)
        return jnp.broadcast_to(line, (8, rows))

    def grads_of(column):
        span = pl.ds(pl.multiple_of(column * width, width), width)
        return dot(hg_buf[...], win_buf[span, :], NT)

    def o_pair(r):
        return pltpu.make_async_remote_copy(
            src_ref=pair_send.at[r], dst_ref=pair_recv.at[r],
            send_sem=os_sem.at[r], recv_sem=or_sem.at[r],
            device_id={"seq": partner}, device_id_type=MESH,
        )

    def o_z(p, way):
        return pltpu.make_async_remote_copy(
            src_ref=z_send.at[p], dst_ref=z_recv.at[way, p],
            send_sem=oz_ssem.at[p], recv_sem=oz_rsem.at[way, p],
            device_id={"tensor": z_to(way)}, device_id_type=MESH,
        )

    def send_sum(p, way, total):
        z_send[p] = total.astype(BF16)
        o_z(p, way).start()

    def s_pair():
        return pltpu.make_async_remote_copy(
            src_ref=sc_pair.at[0], dst_ref=sc_pair.at[1],
            send_sem=ss_sem.at[0], recv_sem=sr_sem.at[0],
            device_id={"seq": partner}, device_id_type=MESH,
        )

    def s_z(r):
        return pltpu.make_async_remote_copy(
            src_ref=sc_z.at[0], dst_ref=sc_z.at[r],
            send_sem=ss_sem.at[r], recv_sem=sr_sem.at[r],
            device_id={"tensor": t_out(r)}, device_id_type=MESH,
        )

    order = []
    for i in range((nt + 1) // 2):
        order += [nt - 1 - i] if nt - 1 - i == i else [nt - 1 - i, i]

    sc_pair[0] = upstream(other)
    s_pair().start()
    for p in order:
        pair_send[p] = grads_of(p).astype(BF16)
        o_pair(p).start()

    mine = upstream(k)
    s_pair().wait_recv()
    sc_z[0] = mine + sc_pair[1]
    for r in range(1, nt):
        s_z(r).start()
    for p in order:
        keep[p] = grads_of(p)
        o_pair(p).wait_recv()
        keep[p] += pair_recv[p].astype(F32)
        if p > 0:
            @pl.when(t == 0)
            def _():
                send_sum(p, 0, keep[p])
        if p < nt - 1:
            @pl.when(t == nt - 1)
            def _():
                send_sum(p, 1, keep[p])
    for p in order:
        @pl.when((t > 0) & (t < p))
        def _():
            o_z(p, 0).wait_recv()
            send_sum(p, 0, keep[p] + z_recv[0, p].astype(F32))

        @pl.when((t < nt - 1) & (t > p))
        def _():
            o_z(p, 1).wait_recv()
            send_sum(p, 1, keep[p] + z_recv[1, p].astype(F32))

    drain_weights(0)
    drain_weights(1)
    drain_tokens(0)
    drain_tokens(1)
    s_pair().wait_send()
    for p in range(nt):
        o_pair(p).wait_send()
    for r in range(1, nt):
        s_z(r).wait()
    total = sc_z[0]
    for r in range(1, nt):
        total = total + sc_z[r]
    score_ref[...] = total
    for p in range(nt):
        @pl.when(t == p)
        def _():
            if p > 0:
                o_z(p, 0).wait_recv()
                keep[p] += z_recv[0, p].astype(F32)
            if p < nt - 1:
                o_z(p, 1).wait_recv()
                keep[p] += z_recv[1, p].astype(F32)
            rows_ref[...] = keep[p].astype(BF16)

        @pl.when(t != p)
        def _():
            o_z(p, 0).wait_send()


def scatter_kernel(count_ref, idx_ref, rows_ref, line_ref, score_ref, grad_ref, out_ref):
    tile = grad_ref.shape[0]
    slots = idx_ref.shape[1]
    live = lax.broadcasted_iota(jnp.int32, (1, slots), 1) < count_ref[0] * BLK
    picked = jnp.where(live, idx_ref[...], -1)
    spots = lax.broadcasted_iota(jnp.int32, (tile, slots), 0) + pl.program_id(0) * tile
    hot = jnp.where(spots == picked, 1.0, 0.0).astype(BF16)
    scale = jnp.transpose(jnp.broadcast_to(score_ref[...], (128, tile)))[:, :1]
    grad_ref[...] = (dot(hot, rows_ref[...], NN) * scale).astype(BF16)
    rest = jnp.broadcast_to(line_ref[:1, :], (16, slots))
    total = jnp.zeros((16, tile), F32)
    for _ in range(3):
        head = rest.astype(BF16)
        total = total + dot(head, hot, NT)
        rest = rest - head.astype(F32)
    out_ref[...] = total[:1, :]


def per_device(n, nt, inputs, out_grad, router_score, route_index, block_count, w_in, w_out):
    toks, width = inputs.shape
    rows = route_index.shape[1]
    depth, ff = w_in.shape
    half = ff // 2
    dim = width * nt
    chips = n // 2
    dma = pltpu.SemaphoreType.DMA
    vm = pl.BlockSpec(memory_space=pltpu.VMEM)
    hbm = pl.BlockSpec(memory_space=pl.ANY)
    row_grads, lines = pl.pallas_call(
        functools.partial(heavy_kernel, n, nt),
        out_shape=(
            jax.ShapeDtypeStruct((rows, width), BF16),
            jax.ShapeDtypeStruct((8, rows), F32),
        ),
        in_specs=[vm, hbm, hbm, hbm, hbm],
        out_specs=(vm, vm),
        scratch_shapes=[
            pltpu.VMEM((2, toks, width), BF16),
            pltpu.VMEM((2, rows, dim), BF16),
            pltpu.VMEM((2, rows, dim), BF16),
            pltpu.VMEM((n * depth, half), BF16),
            pltpu.VMEM((n, half, depth), BF16),
            pltpu.VMEM((2, rows, half), BF16),
            pltpu.VMEM((2, rows, half), F32),
            pltpu.VMEM((rows, half), BF16),
            pltpu.VMEM((nt, rows, width), BF16),
            pltpu.VMEM((nt, rows, width), BF16),
            pltpu.VMEM((nt, rows, width), BF16),
            pltpu.VMEM((2, nt, rows, width), BF16),
            pltpu.VMEM((rows, width), F32),
            pltpu.VMEM((nt, rows, width), F32),
            pltpu.VMEM((rows, 128), F32),
            pltpu.VMEM((2, 8, rows), F32),
            pltpu.VMEM((nt, 8, rows), F32),
            dma((2,)), dma((2,)),
            dma((2, chips, 2)), dma((2, chips, 2)),
            dma((2, 2, nt)), dma((2, 2, nt)),
            dma((2, 2, nt)), dma((2, 2, nt)),
            dma((nt,)), dma((nt,)),
            dma((nt,)), dma((2, nt)),
            dma((nt,)), dma((nt,)),
        ],
        compiler_params=pltpu.CompilerParams(
            collective_id=0, has_side_effects=True, vmem_limit_bytes=58 * 2**20
        ),
        name="heavy",
    )(route_index, inputs, out_grad, w_in, w_out)

    tile = min(1024, toks)
    input_grad, score_grad = pl.pallas_call(
        scatter_kernel,
        grid=(toks // tile,),
        out_shape=(
            jax.ShapeDtypeStruct((toks, width), BF16),
            jax.ShapeDtypeStruct((1, toks), F32),
        ),
        in_specs=[
            pl.BlockSpec(memory_space=pltpu.SMEM),
            pl.BlockSpec((1, rows), lambda i: (0, 0)),
            pl.BlockSpec((rows, width), lambda i: (0, 0)),
            pl.BlockSpec((8, rows), lambda i: (0, 0)),
            pl.BlockSpec((1, tile), lambda i: (0, i)),
        ],
        out_specs=(
            pl.BlockSpec((tile, width), lambda i: (i, 0)),
            pl.BlockSpec((1, tile), lambda i: (0, i)),
        ),
        compiler_params=pltpu.CompilerParams(vmem_limit_bytes=32 * 2**20),
        name="scatter",
    )(block_count, route_index, row_grads, lines, router_score.reshape(1, toks))
    return input_grad, score_grad.reshape(toks)


def solution(mesh):
    placed = (
        P("seq", "tensor"),
        P("seq", "tensor"),
        P("seq"),
        P("seq", None),
        P("seq"),
        P("seq", "tensor"),
        P("tensor", "seq"),
    )
    return jax.shard_map(
        functools.partial(per_device, mesh.shape["seq"], mesh.shape["tensor"]),
        mesh=mesh,
        in_specs=placed,
        out_specs=(P("seq", "tensor"), P("seq")),
        check_vma=False,
    )
```

```python
import functools

import jax
import jax.numpy as jnp
from jax import lax
from jax.experimental import pallas as pl
from jax.experimental.pallas import tpu as pltpu
from jax.sharding import PartitionSpec as P

BLK = 128
MESH = pl.DeviceIdType.MESH
F32, BF16 = jnp.float32, jnp.bfloat16
NT = (((1,), (1,)), ((), ()))
NN = (((1,), (0,)), ((), ()))

gelu_coeff = 0.7978845608028654
cubic_coeff = 0.044715


def gelu_pair(values):
    square = values * values
    tangent = jnp.tanh(gelu_coeff * (values + cubic_coeff * square * values))
    half = 0.5 * (1.0 + tangent)
    slope = half + 0.5 * values * (1.0 - tangent * tangent) * gelu_coeff * (
        1.0 + 3.0 * cubic_coeff * square
    )
    return values * half, slope


def dot(a, b, dims):
    return lax.dot_general(a, b, dims, preferred_element_type=F32)


def heavy_kernel(
    n, nt, idx_ref, inputs_ref, grads_ref, win_ref, wout_ref, rows_ref, score_ref,
    tok_buf, x_buf, g_buf, win_buf, wout_buf, act_buf, slope_buf, hg_buf,
    pair_send, pair_recv, z_send, z_recv, own_buf, keep, sc_out, sc_own, sc_pair, sc_z,
    tok_sem, wl_sem, w_send, w_recv, z_ssem, z_rsem, p_ssem, p_rsem,
    os_sem, or_sem, oz_ssem, oz_rsem, ss_sem, sr_sem,
):
    s, t = lax.axis_index("seq"), lax.axis_index("tensor")
    c, k = lax.div(s, 2), lax.rem(s, 2)
    chips = n // 2
    toks, width = inputs_ref.shape
    rows = idx_ref.shape[1]
    depth = win_ref.shape[0]
    half = win_ref.shape[1] // 2
    other = 1 - k
    partner = c * 2 + other
    square = chips == 4

    if square:
        out_chip = [c + 1 - 2 * lax.rem(c, 2), lax.rem(c + 2, 4), 3 - c]
        in_chip = out_chip
    else:
        out_chip = [lax.rem(c + r, chips) for r in range(1, chips)]
        in_chip = [lax.rem(c + chips - r, chips) for r in range(1, chips)]

    def t_out(r):
        return lax.rem(t + r, nt)

    load = [
        pltpu.make_async_copy(src, tok_buf.at[i], tok_sem.at[i])
        for i, src in enumerate((inputs_ref, grads_ref))
    ]
    for cp in load:
        cp.start()

    def weight_src(w, core):
        start = pl.multiple_of(core * half, half)
        if w == 0:
            return win_ref.at[:, pl.ds(start, half)]
        return wout_ref.at[pl.ds(start, half), :]

    def weight_dst(w, owner):
        if w == 0:
            return win_buf.at[pl.ds(pl.multiple_of(owner * depth, depth), depth), :]
        return wout_buf.at[owner]

    local = [
        pltpu.make_async_copy(weight_src(w, k), weight_dst(w, s), wl_sem.at[w]) for w in range(2)
    ]
    for cp in local:
        cp.start()

    barrier = pltpu.get_barrier_semaphore()
    for chip in out_chip:
        for core in range(2):
            pl.semaphore_signal(
                barrier, inc=1, device_id={"seq": chip * 2 + core}, device_id_type=MESH
            )
    pl.semaphore_signal(barrier, inc=1, device_id={"seq": partner}, device_id_type=MESH)
    for r in range(1, nt):
        pl.semaphore_signal(barrier, inc=1, device_id={"tensor": t_out(r)}, device_id_type=MESH)
    pl.semaphore_wait(barrier, 2 * (chips - 1) + 1 + nt - 1)

    def weight_copy(w, r, q):
        core = k if q == 0 else other
        return pltpu.make_async_remote_copy(
            src_ref=weight_src(w, core), dst_ref=weight_dst(w, s),
            send_sem=w_send.at[w, r, q], recv_sem=w_recv.at[w, r, q],
            device_id={"seq": out_chip[r] * 2 + core}, device_id_type=MESH,
        )

    def weight_hop(w, q):
        came, go = (0, 1) if q == 0 else (1, 0)
        owner = in_chip[came] * 2 + (k if q == 0 else other)
        return pltpu.make_async_remote_copy(
            src_ref=weight_dst(w, owner), dst_ref=weight_dst(w, owner),
            send_sem=w_send.at[w, 2, q], recv_sem=w_recv.at[w, 2, q],
            device_id={"seq": out_chip[go] * 2 + k}, device_id_type=MESH,
        )

    def weight_landed(w, r, q):
        owner = in_chip[r] * 2 + (k if q == 0 else other)
        return pltpu.make_async_remote_copy(
            src_ref=weight_dst(w, owner), dst_ref=weight_dst(w, owner),
            send_sem=w_send.at[w, r, q], recv_sem=w_recv.at[w, r, q],
            device_id={"seq": owner}, device_id_type=MESH,
        )

    def weight_pair(w, owner):
        return pltpu.make_async_remote_copy(
            src_ref=weight_src(w, other), dst_ref=weight_dst(w, owner),
            send_sem=w_send.at[w, chips - 1, 0], recv_sem=w_recv.at[w, chips - 1, 0],
            device_id={"seq": partner}, device_id_type=MESH,
        )

    direct = range(2) if square else range(chips - 1)

    def start_weights(w):
        for q in range(2):
            for r in direct:
                weight_copy(w, r, q).start()
        weight_pair(w, s).start()

    def pass_weights(w):
        if square:
            for q in range(2):
                weight_landed(w, q, q).wait_recv()
                weight_hop(w, q).start()

    def finish_weights(w):
        local[w].wait()
        weight_pair(w, partner).wait_recv()
        for r in range(chips - 1):
            for q in range(2):
                if square and r == q:
                    continue
                weight_landed(w, r, q).wait_recv()

    def drain_weights(w):
        weight_pair(w, s).wait_send()
        for q in range(2):
            for r in direct:
                weight_copy(w, r, q).wait_send()
            if square:
                weight_hop(w, q).wait_send()

    tokens = (x_buf, g_buf)

    def piece(v, shard, column):
        return tokens[v].at[shard, :, pl.ds(pl.multiple_of(column * width, width), width)]

    def gather(v):
        load[v].wait()
        step = min(512, toks)
        column = jnp.transpose(jnp.broadcast_to(idx_ref[...], (128, rows)))[:, :1]
        dst = piece(v, k, t)
        total = jnp.zeros((rows, width), F32)
        x_own = own_buf

        x_own[...] = total

        def body(i, carry):
            start = pl.multiple_of(i * step, step)
            spots = lax.broadcasted_iota(jnp.int32, (rows, step), 1) + i * step
            hot = jnp.where(column == spots, 1.0, 0.0).astype(BF16)
            x_own[...] += dot(hot, tok_buf[v, pl.ds(start, step), :], NN)
            return carry

        lax.fori_loop(0, toks // step, body, 0)
        dst[...] = x_own[...].astype(BF16)

    def origin(way, d):
        return lax.rem(t + nt - d, nt) if way == 0 else lax.rem(t + d, nt)

    def has(way, d):
        return t >= d if way == 0 else t + d < nt

    def z_to(way):
        return lax.rem(t + 1, nt) if way == 0 else lax.rem(t + nt - 1, nt)

    def z_copy(v, way, d):
        ref = piece(v, k, origin(way, d))
        return pltpu.make_async_remote_copy(
            src_ref=ref, dst_ref=ref,
            send_sem=z_ssem.at[v, way, d], recv_sem=z_rsem.at[v, way, d + 1],
            device_id={"tensor": z_to(way)}, device_id_type=MESH,
        )

    def z_landed(v, way, d):
        ref = piece(v, k, origin(way, d))
        return pltpu.make_async_remote_copy(
            src_ref=ref, dst_ref=ref,
            send_sem=z_ssem.at[v, way, d], recv_sem=z_rsem.at[v, way, d],
            device_id={"tensor": z_to(1 - way)}, device_id_type=MESH,
        )

    def pair_copy(v, way, d, shard):
        ref = piece(v, shard, origin(way, d))
        return pltpu.make_async_remote_copy(
            src_ref=ref, dst_ref=ref,
            send_sem=p_ssem.at[v, way, d], recv_sem=p_rsem.at[v, way, d],
            device_id={"seq": partner}, device_id_type=MESH,
        )

    def start_tokens(v):
        for way in range(2):
            @pl.when(has(1 - way, 1))
            def _():
                z_copy(v, way, 0).start()
        pair_copy(v, 0, 0, k).start()

    def pass_tokens(v, d):
        for way in range(2):
            @pl.when(has(way, d))
            def _():
                z_landed(v, way, d).wait_recv()
                if d < nt - 1:
                    @pl.when(has(1 - way, 1))
                    def _():
                        z_copy(v, way, d).start()
                pair_copy(v, way, d, k).start()

    def finish_tokens(v):
        pair_copy(v, 0, 0, other).wait_recv()
        for way in range(2):
            for d in range(1, nt):
                @pl.when(has(way, d))
                def _():
                    pair_copy(v, way, d, other).wait_recv()

    def drain_tokens(v):
        pair_copy(v, 0, 0, k).wait_send()
        for way in range(2):
            for d in range(nt - 1):
                @pl.when(has(way, d) & has(1 - way, 1))
                def _():
                    z_copy(v, way, d).wait_send()
            for d in range(1, nt):
                @pl.when(has(way, d))
                def _():
                    pair_copy(v, way, d, k).wait_send()

    start_weights(0)
    gather(0)
    start_tokens(0)
    gather(1)
    start_tokens(1)
    pass_tokens(0, 1)
    pass_weights(0)
    start_weights(1)
    for d in range(2, nt):
        if d < nt - 1:
            pass_tokens(0, d)
        pass_tokens(1, d - 1)
    pass_weights(1)
    pass_tokens(0, nt - 1)
    finish_weights(0)
    finish_tokens(0)

    ft = min(256, half)

    def hidden_step(i, carry):
        shard, f = lax.div(i, half // ft), lax.rem(i, half // ft)
        cols = pl.ds(pl.multiple_of(f * ft, ft), ft)
        hidden = dot(x_buf[shard], win_buf[:, cols], NN)
        forward, slope = gelu_pair(hidden)
        act_buf[shard, :, cols] = forward.astype(BF16)
        slope_buf[shard, :, cols] = slope
        return carry

    lax.fori_loop(0, 2 * (half // ft), hidden_step, 0)

    pass_tokens(1, nt - 1)
    finish_weights(1)
    finish_tokens(1)

    hr = rows // 2
    own_rows = pl.ds(pl.multiple_of(k * hr, hr), hr)
    other_rows = pl.ds(pl.multiple_of(other * hr, hr), hr)

    def upstream(h):
        span = pl.ds(h * hr, hr)
        sc_out[...] = jnp.zeros_like(sc_out)

        def both(ref, cols):
            return jnp.concatenate([ref[0, span, cols], ref[1, span, cols]], axis=0)

        def step(f, carry):
            cols = pl.ds(pl.multiple_of(f * ft, ft), ft)
            weights = jnp.concatenate([wout_buf[i, cols, :] for i in range(n)], axis=1)
            up = dot(both(g_buf, slice(None)), weights, NT)
            hg_buf[:, cols] = (up * both(slope_buf, cols)).astype(BF16)
            terms = up * both(act_buf, cols).astype(F32)
            part = terms[:, :128]
            for i in range(1, ft // 128):
                part = part + terms[:, i * 128:(i + 1) * 128]
            sc_out[...] += part
            return carry

        lax.fori_loop(0, half // ft, step, 0)
        line = jnp.sum(jnp.transpose(sc_out[...]), axis=0, keepdims=True)
        for shard in range(2):
            sc_own[shard, :, span] = jnp.broadcast_to(line[:, shard * hr:(shard + 1) * hr], (8, hr))

    def grads_of(column):
        span = pl.ds(column * width, width)
        return dot(hg_buf[...], win_buf[span, :], NT)

    def o_pair(h, p):
        span = pl.ds(h * hr, hr)
        return pltpu.make_async_remote_copy(
            src_ref=pair_send.at[p, span, :], dst_ref=pair_recv.at[p, span, :],
            send_sem=os_sem.at[h, p], recv_sem=or_sem.at[h, p],
            device_id={"seq": partner}, device_id_type=MESH,
        )

    def o_z(h, p, way):
        span = pl.ds(h * hr, hr)
        return pltpu.make_async_remote_copy(
            src_ref=z_send.at[p, span, :], dst_ref=z_recv.at[way, p, span, :],
            send_sem=oz_ssem.at[h, p], recv_sem=oz_rsem.at[h, way, p],
            device_id={"tensor": z_to(way)}, device_id_type=MESH,
        )

    def arrived(h, p, way):
        o_z(h, p, way).wait_recv()
        return z_recv[way, p, h * hr:(h + 1) * hr, :].astype(F32)

    def send_sum(h, p, way, total):
        z_send[p, h * hr:(h + 1) * hr, :] = total.astype(BF16)
        o_z(h, p, way).start()

    def s_pair():
        return pltpu.make_async_remote_copy(
            src_ref=sc_pair.at[0], dst_ref=sc_pair.at[1],
            send_sem=ss_sem.at[0], recv_sem=sr_sem.at[0],
            device_id={"seq": partner}, device_id_type=MESH,
        )

    def s_z(r):
        return pltpu.make_async_remote_copy(
            src_ref=sc_z.at[0], dst_ref=sc_z.at[r],
            send_sem=ss_sem.at[r], recv_sem=sr_sem.at[r],
            device_id={"tensor": t_out(r)}, device_id_type=MESH,
        )

    order = []
    for i in range((nt + 1) // 2):
        order += [nt - 1 - i] if nt - 1 - i == i else [nt - 1 - i, i]

    def make(h, p):
        keep[h, p] = grads_of(p)
        pair_send[p, h * hr:(h + 1) * hr, :] = keep[h, p, other_rows, :].astype(BF16)
        o_pair(h, p).start()

    def add_pair(h, p):
        o_pair(h, p).wait_recv()
        keep[h, p, own_rows, :] += pair_recv[p, h * hr:(h + 1) * hr, :].astype(F32)
        if p > 0:
            @pl.when(t == 0)
            def _():
                send_sum(h, p, 0, keep[h, p, own_rows, :])
        if p < nt - 1:
            @pl.when(t == nt - 1)
            def _():
                send_sum(h, p, 1, keep[h, p, own_rows, :])

    def hop(h, p):
        @pl.when((t > 0) & (t < p))
        def _():
            send_sum(h, p, 0, keep[h, p, own_rows, :] + arrived(h, p, 0))

        @pl.when((t < nt - 1) & (t > p))
        def _():
            send_sum(h, p, 1, keep[h, p, own_rows, :] + arrived(h, p, 1))

    for h in range(2):
        upstream(h)
        if h == 1:
            for p in order[:2]:
                hop(0, p)
        make(h, order[0])
        for before, p in zip(order, order[1:]):
            make(h, p)
            add_pair(h, before)
        add_pair(h, order[-1])

    sc_pair[0] = sc_own[other]
    s_pair().start()
    for p in order[2:]:
        hop(0, p)
    s_pair().wait_recv()
    sc_z[0] = sc_own[k] + sc_pair[1]
    for r in range(1, nt):
        s_z(r).start()
    for p in order:
        hop(1, p)

    drain_weights(0)
    drain_weights(1)
    drain_tokens(0)
    drain_tokens(1)
    s_pair().wait_send()
    for r in range(1, nt):
        s_z(r).wait()
    total = sc_z[0]
    for r in range(1, nt):
        total = total + sc_z[r]
    score_ref[...] = total
    for h in range(2):
        for p in range(nt):
            o_pair(h, p).wait_send()

            @pl.when(t == p)
            def _():
                if p > 0:
                    keep[h, p, own_rows, :] += arrived(h, p, 0)
                if p < nt - 1:
                    keep[h, p, own_rows, :] += arrived(h, p, 1)
                rows_ref[h * hr:(h + 1) * hr, :] = keep[h, p, own_rows, :].astype(BF16)

            @pl.when(t != p)
            def _():
                o_z(h, p, 0).wait_send()


def scatter_kernel(count_ref, idx_ref, rows_ref, line_ref, score_ref, grad_ref, out_ref):
    tile = grad_ref.shape[0]
    slots = idx_ref.shape[1]
    live = lax.broadcasted_iota(jnp.int32, (1, slots), 1) < count_ref[0] * BLK
    picked = jnp.where(live, idx_ref[...], -1)
    spots = lax.broadcasted_iota(jnp.int32, (tile, slots), 0) + pl.program_id(0) * tile
    hot = jnp.where(spots == picked, 1.0, 0.0).astype(BF16)
    scale = jnp.transpose(jnp.broadcast_to(score_ref[...], (128, tile)))[:, :1]
    grad_ref[...] = (dot(hot, rows_ref[...], NN) * scale).astype(BF16)
    rest = jnp.broadcast_to(line_ref[:1, :], (16, slots))
    total = jnp.zeros((16, tile), F32)
    for _ in range(3):
        head = rest.astype(BF16)
        total = total + dot(head, hot, NT)
        rest = rest - head.astype(F32)
    out_ref[...] = total[:1, :]


def per_device(n, nt, inputs, out_grad, router_score, route_index, block_count, w_in, w_out):
    toks, width = inputs.shape
    rows = route_index.shape[1]
    depth, ff = w_in.shape
    half = ff // 2
    dim = width * nt
    chips = n // 2
    dma = pltpu.SemaphoreType.DMA
    vm = pl.BlockSpec(memory_space=pltpu.VMEM)
    hbm = pl.BlockSpec(memory_space=pl.ANY)
    row_grads, lines = pl.pallas_call(
        functools.partial(heavy_kernel, n, nt),
        out_shape=(
            jax.ShapeDtypeStruct((rows, width), BF16),
            jax.ShapeDtypeStruct((8, rows), F32),
        ),
        in_specs=[vm, hbm, hbm, hbm, hbm],
        out_specs=(vm, vm),
        scratch_shapes=[
            pltpu.VMEM((2, toks, width), BF16),
            pltpu.VMEM((2, rows, dim), BF16),
            pltpu.VMEM((2, rows, dim), BF16),
            pltpu.VMEM((n * depth, half), BF16),
            pltpu.VMEM((n, half, depth), BF16),
            pltpu.VMEM((2, rows, half), BF16),
            pltpu.VMEM((2, rows, half), F32),
            pltpu.VMEM((rows, half), BF16),
            pltpu.VMEM((nt, rows, width), BF16),
            pltpu.VMEM((nt, rows, width), BF16),
            pltpu.VMEM((nt, rows, width), BF16),
            pltpu.VMEM((2, nt, rows, width), BF16),
            pltpu.VMEM((rows, width), F32),
            pltpu.VMEM((2, nt, rows, width), F32),
            pltpu.VMEM((rows, 128), F32),
            pltpu.VMEM((2, 8, rows), F32),
            pltpu.VMEM((2, 8, rows), F32),
            pltpu.VMEM((nt, 8, rows), F32),
            dma((2,)), dma((2,)),
            dma((2, chips, 2)), dma((2, chips, 2)),
            dma((2, 2, nt)), dma((2, 2, nt)),
            dma((2, 2, nt)), dma((2, 2, nt)),
            dma((2, nt)), dma((2, nt)),
            dma((2, nt)), dma((2, 2, nt)),
            dma((nt,)), dma((nt,)),
        ],
        compiler_params=pltpu.CompilerParams(
            collective_id=0, has_side_effects=True, vmem_limit_bytes=58 * 2**20
        ),
        name="heavy",
    )(route_index, inputs, out_grad, w_in, w_out)

    tile = min(1024, toks)
    input_grad, score_grad = pl.pallas_call(
        scatter_kernel,
        grid=(toks // tile,),
        out_shape=(
            jax.ShapeDtypeStruct((toks, width), BF16),
            jax.ShapeDtypeStruct((1, toks), F32),
        ),
        in_specs=[
            pl.BlockSpec(memory_space=pltpu.SMEM),
            pl.BlockSpec((1, rows), lambda i: (0, 0)),
            pl.BlockSpec((rows, width), lambda i: (0, 0)),
            pl.BlockSpec((8, rows), lambda i: (0, 0)),
            pl.BlockSpec((1, tile), lambda i: (0, i)),
        ],
        out_specs=(
            pl.BlockSpec((tile, width), lambda i: (i, 0)),
            pl.BlockSpec((1, tile), lambda i: (0, i)),
        ),
        compiler_params=pltpu.CompilerParams(vmem_limit_bytes=32 * 2**20),
        name="scatter",
    )(block_count, route_index, row_grads, lines, router_score.reshape(1, toks))
    return input_grad, score_grad.reshape(toks)


def solution(mesh):
    placed = (
        P("seq", "tensor"),
        P("seq", "tensor"),
        P("seq"),
        P("seq", None),
        P("seq"),
        P("seq", "tensor"),
        P("tensor", "seq"),
    )
    return jax.shard_map(
        functools.partial(per_device, mesh.shape["seq"], mesh.shape["tensor"]),
        mesh=mesh,
        in_specs=placed,
        out_specs=(P("seq", "tensor"), P("seq")),
        check_vma=False,
    )
```
